32 devices in a mesh: freq: 2 (over x), shot: 8 (over z, y), rcv: 2 (over core).
Axes of the slice: x: 2, y: 2, z: 4, core: 2. Of those that a mesh axis runs over, the one named last changes fastest.
Arguments:
- data_left: float32 [2, 8192, 512], P(None, ('freq', 'shot'), 'rcv'), parts along dimension 1, may hold values from -6 to 6
- slab_table: float32 [2, 2048, 2048], P(None, ('freq', 'shot'), 'rcv'), parts along dimension 1, may hold values from -0.1875 to 0.1875
- recorded: float32 [2, 8192, 2048], P(None, ('freq', 'shot'), 'rcv'), parts along dimension 1, may hold values from -6 to 6
- filter_bank: float32 [16, 17], replicated, may hold values from -1.75 to 1.75
- row_taps: int32 [32], P('shot'), may hold values from 0 to 15
- row_start: int32 [32], P('shot'), may hold values from 0 to 4
- col_taps: int32 [16], P('rcv'), may hold values from 0 to 15
- col_start: int32 [16], P('rcv'), may hold values from 0 to 4
- panel_owner: int32 [8], replicated, may hold values from 0 to 7, each once
- shrink_level: float32 [2048], P('rcv'), may hold values from 0.1 to 0.8
Outputs:
- primaries: float32 [2, 8192, 2048], P(None, ('freq', 'shot'), 'rcv'), parts along dimension 1
The draws below stay inside these ranges and needn't reach their ends.
There are 2 independent parts, one for each index of `freq`. The reference program is written for one: setup_inputs(seed, part) draws one part's arguments, and reference() takes and returns one part's arrays. A program takes and returns all parts, laid end to end along the dimension named above; an argument that names none is the same for every part. Nothing has to cross between parts.
Inputs may be any that keep to these rules, and one draw needn't show every extreme that they name: `panel_owner`: each shot index appears once.
All inputs are finite; a program needn't handle non-finite values.
Results may differ from the reference program's by a relative error of at most 0.0001.
Values sent between devices are 32-bit elements; how exact they have to be, the bound alone decides.
A program may use at most 64 MiB of HBM per device.

```python
import math
import jax
import jax.numpy as jnp
from jax import lax

PANEL = 128
PANELS = 4
TAPS = 17
WIN = 13
NBANK = 16
TBLK = 128
HALO = 8
SHOTS = 4096
RECV = 2048
KSUM = 512
SLABS = 1024
N_SHOT = 8


def place_ends(result, own_key, low, high):
    place = [jax.random.randint(jax.random.fold_in(own_key, axis), (), 0, length) for axis, length in enumerate(result.shape)]
    widest = result.shape.index(max(result.shape))
    neighbour = place[:widest] + [(place[widest] + 1) % result.shape[widest]] + place[widest + 1:]
    return result.at[tuple(place)].set(low).at[tuple(neighbour)].set(high)


def level_of(stream_key, shape, split, least, high):
    loudness = 1.0
    for axis_at, shards_of in split:
        draws = jax.random.uniform(jax.random.fold_in(jax.random.fold_in(stream_key, 6), axis_at), (shards_of,), jnp.float32, least / len(split), high / len(split))
        loudness = loudness * jnp.repeat(jnp.exp(draws), shape[axis_at] // shards_of).reshape((-1,) + (1,) * (len(shape) - 1 - axis_at))
    return loudness


def scatter_about(key, dims, scale, bound, shards=(), held_as=jnp.bfloat16):
    loudness = level_of(key, dims, shards, -0.22, 0.18) if shards else 1.0
    entries = jax.random.normal(key, dims, jnp.float32) * scale * loudness
    return jnp.minimum(jnp.maximum(entries, -bound), bound).astype(held_as)


def setup_inputs(seed: int = 0, part: int = 0) -> dict:
    keys = jax.random.split(jax.random.key(seed), 11)
    part_keys = jax.random.split(jax.random.fold_in(keys[10], part), 11)
    data_left = scatter_about(part_keys[0], (2, SHOTS, KSUM), 1.0, 6.0, ((1, 8), (2, 2)), jnp.float32)
    slab_table = scatter_about(part_keys[1], (2, SLABS, RECV), (2 * KSUM) ** -0.5, 0.1875, ((1, 8), (2, 2)), jnp.float32)
    recorded = scatter_about(part_keys[2], (2, SHOTS, RECV), 1.0, 6.0, ((1, 8), (2, 2)), jnp.float32)
    filter_bank = scatter_about(keys[3], (NBANK, TAPS), WIN ** -0.5, 1.75, (), jnp.float32)
    row_taps = place_ends(jax.random.randint(keys[4], (SHOTS // TBLK,), 0, NBANK), jax.random.fold_in(keys[4], 1), 0, NBANK - 1).astype(jnp.int32)
    row_start = place_ends(jax.random.randint(keys[5], (SHOTS // TBLK,), 0, TAPS - WIN + 1), jax.random.fold_in(keys[5], 1), 0, TAPS - WIN).astype(jnp.int32)
    col_taps = place_ends(jax.random.randint(keys[6], (RECV // TBLK,), 0, NBANK), jax.random.fold_in(keys[6], 1), 0, NBANK - 1).astype(jnp.int32)
    col_start = place_ends(jax.random.randint(keys[7], (RECV // TBLK,), 0, TAPS - WIN + 1), jax.random.fold_in(keys[7], 1), 0, TAPS - WIN).astype(jnp.int32)
    panel_owner = jax.random.permutation(keys[8], N_SHOT).astype(jnp.int32)
    shrink_level = jnp.clip(jnp.exp(math.log(0.8) - 2.0794415 * jax.random.uniform(keys[9], (RECV,), jnp.float32) ** level_of(keys[9], (RECV,), ((0, 2),), -0.2, 0.2)), 0.1, 0.8)
    return dict(data_left=data_left, slab_table=slab_table, recorded=recorded, filter_bank=filter_bank, row_taps=row_taps, row_start=row_start, col_taps=col_taps, col_start=col_start, panel_owner=panel_owner, shrink_level=shrink_level)


def block_taps(filter_bank, taps_index, start, block_rows):
    count = filter_bank.shape[0]
    selector = (taps_index[:, None] == jnp.arange(count, dtype=jnp.int32)[None, :]).astype(jnp.float32)
    weights = jnp.dot(selector, filter_bank, preferred_element_type=jnp.float32, precision=lax.Precision.HIGHEST)
    tap_index = jnp.arange(TAPS, dtype=jnp.int32)[None, :]
    inside = (tap_index >= start[:, None]) & (tap_index < start[:, None] + WIN)
    weights = jnp.where(inside, weights, jnp.float32(0.0))
    return jnp.repeat(weights, block_rows, axis=0)

def filter_rows(extended, weights, length):
    total = jnp.zeros((2, length, extended.shape[2]), jnp.float32)
    for tap in range(TAPS):
        total = total + weights[:, tap][None, :, None] * extended[:, tap:tap + length, :]
    return total

def filter_cols(extended, weights, length):
    total = jnp.zeros((2, extended.shape[1], length), jnp.float32)
    for tap in range(TAPS):
        total = total + weights[:, tap][None, None, :] * extended[:, :, tap:tap + length]
    return total

def complex_product(left, right):
    high = lax.Precision.HIGHEST
    real_part = jnp.dot(left[0], right[0], preferred_element_type=jnp.float32, precision=high) - jnp.dot(left[1], right[1], preferred_element_type=jnp.float32, precision=high)
    imag_part = jnp.dot(left[0], right[1], preferred_element_type=jnp.float32, precision=high) + jnp.dot(left[1], right[0], preferred_element_type=jnp.float32, precision=high)
    return jnp.stack([real_part, imag_part])

def soft_shrink(recorded, matched, shrink_level):
    residual = recorded - matched
    magnitude = jnp.sqrt(residual[0] * residual[0] + residual[1] * residual[1])
    level = shrink_level[None, :]
    factor = jnp.maximum(magnitude - level, jnp.float32(0.0)) / jnp.maximum(magnitude, level)
    return residual * factor[None]

def reference(data_left, slab_table, recorded, filter_bank, row_taps, row_start, col_taps, col_start, panel_owner, shrink_level):
    shots = data_left.shape[1]
    receivers = slab_table.shape[2]
    predicted = jnp.zeros((2, shots, receivers), jnp.float32)
    for panel in range(PANELS):
        left = data_left[:, :, panel * PANEL:(panel + 1) * PANEL]
        first = (panel_owner[panel] * PANEL).astype(jnp.int32)
        right = lax.dynamic_slice_in_dim(slab_table, first, PANEL, 1)
        predicted = predicted + complex_product(left, right)
    row_weights = block_taps(filter_bank, row_taps, row_start, TBLK)
    col_weights = block_taps(filter_bank, col_taps, col_start, TBLK)
    padded = jnp.pad(predicted, ((0, 0), (HALO, HALO), (0, 0)))
    row_filtered = filter_rows(padded, row_weights, shots)
    padded = jnp.pad(row_filtered, ((0, 0), (0, 0), (HALO, HALO)))
    matched = filter_cols(padded, col_weights, receivers)
    return soft_shrink(recorded, matched, shrink_level)
```

```python
import functools

import jax
import jax.numpy as jnp
from jax import lax
from jax.experimental import pallas as pl
from jax.experimental.pallas import tpu as pltpu
from jax.sharding import PartitionSpec as P

PANEL = 128
PANELS = 4
TAPS = 17
WIN = 13
TBLK = 128
HALO = 8
HOP = 2
SIDE = 2
MESH = pl.DeviceIdType.MESH


def taps_of(bank, index, start, block):
    row, first = index[block], start[block]
    return [
        jnp.where((first <= t) & (t < first + WIN), bank[row, t], jnp.float32(0.0))
        for t in range(TAPS)
    ]


def band_of(taps, distance):
    band = jnp.zeros(distance.shape, jnp.float32)
    for t, weight in enumerate(taps):
        band = jnp.where(distance == t, weight, band)
    return band


def split(x):
    high = x.astype(jnp.bfloat16)
    return high, (x - high.astype(jnp.float32)).astype(jnp.bfloat16)


def kernel(
    n, nr, nlo,
    left, slab, recorded, level, bank, row_taps, row_start, col_taps, col_start, owner,
    out,
    ext, lfilt, lhigh, llow, rec, stage, halo, cut, plane, upin, upout, dnin, dnout, full,
    rec_sem, out_sem, lh_send, lh_recv, sh_send, sh_recv, lf_send, lf_recv,
    cut_send, cut_recv, up_send, up_recv, dn_send, dn_recv, side_send, side_recv,
):
    nhi = n // nlo
    shots, width = left.shape[1], left.shape[2]
    columns = slab.shape[2]
    chunks = columns // TBLK
    items = chunks * PANELS
    piece = PANEL // nlo
    s, r = lax.axis_index("shot"), lax.axis_index("rcv")
    h, l = s // nlo, s % nlo

    def at(shot, rcv):
        return (lax.axis_index("freq"), shot, rcv)

    def remote(src, dst, send, recv, shot, rcv):
        return pltpu.make_async_remote_copy(
            src_ref=src, dst_ref=dst, send_sem=send, recv_sem=recv,
            device_id=at(shot, rcv), device_id_type=MESH,
        )

    barrier = pltpu.get_barrier_semaphore()

    def greet(shot, rcv):
        pl.semaphore_signal(barrier, inc=1, device_id=at(shot, rcv), device_id_type=MESH)

    for k in range(1, nr):
        greet(s, (r + k) % nr)
    for k in range(1, nlo):
        greet(h * nlo + (l + k) % nlo, r)
    pl.when(h > 0)(lambda: greet(s - nlo, r))
    pl.when(h < nhi - 1)(lambda: greet(s + nlo, r))
    pl.when(s > 0)(lambda: greet(s - 1, r))
    pl.when(s < n - 1)(lambda: greet(s + 1, r))
    ends = jnp.int32(nr + nlo - 2)
    for near in (h > 0, h < nhi - 1, s > 0, s < n - 1):
        ends = ends + jnp.where(near, 1, 0)
    pl.semaphore_wait(barrier, ends)

    def slab_halo(to, rcv):
        start = columns - TBLK if to == 0 else 0
        return remote(slab.at[:, :, pl.ds(start, TBLK)], halo.at[to], sh_send.at[to], sh_recv.at[to], s, rcv)

    def left_halo(to, shot):
        start = shots - HALO if to == 0 else 0
        place = 0 if to == 0 else shots + HALO
        return remote(
            left.at[:, pl.ds(start, HALO)], ext.at[:, pl.ds(place, HALO)],
            lh_send.at[to], lh_recv.at[to], shot, r,
        )

    pl.when(r < nr - 1)(lambda: slab_halo(0, r + 1).start())
    pl.when(r > 0)(lambda: slab_halo(1, r - 1).start())
    pl.when(s < n - 1)(lambda: left_halo(0, s + 1).start())
    pl.when(s > 0)(lambda: left_halo(1, s - 1).start())
    fetch = pltpu.make_async_copy(recorded, rec, rec_sem)
    fetch.start()

    @pl.when(r == 0)
    def _():
        halo[0] = jnp.zeros(halo.shape[1:], jnp.float32)

    @pl.when(r == nr - 1)
    def _():
        halo[1] = jnp.zeros(halo.shape[1:], jnp.float32)

    @pl.when(s == 0)
    def _():
        ext[:, :HALO] = jnp.zeros((2, HALO, width), jnp.float32)

    @pl.when(s == n - 1)
    def _():
        ext[:, shots + HALO :] = jnp.zeros((2, HALO, width), jnp.float32)

    ext[:, HALO : shots + HALO] = left[...]
    pl.when(r > 0)(lambda: slab_halo(0, r - 1).wait_recv())
    pl.when(r < nr - 1)(lambda: slab_halo(1, r + 1).wait_recv())

    def lanes(c):
        return pl.ds(pl.multiple_of(c * TBLK, TBLK), TBLK)

    def cut_copy(c, there, sender):
        return remote(
            cut.at[c, there], plane.at[c, sender], cut_send.at[c, there], cut_recv.at[c, sender],
            h * nlo + there, r,
        )

    def filter_slab(c):
        before = jnp.where(c > 0, slab[:, :, lanes(jnp.maximum(c - 1, 0))], halo[0])
        after = jnp.where(c < chunks - 1, slab[:, :, lanes(jnp.minimum(c + 1, chunks - 1))], halo[1])
        whole = jnp.concatenate([before, slab[:, :, lanes(c)], after], axis=2)
        shape = (3 * TBLK, TBLK)
        distance = (
            lax.broadcasted_iota(jnp.int32, shape, 0) - lax.broadcasted_iota(jnp.int32, shape, 1) - (TBLK - HALO)
        )
        band = band_of(taps_of(bank, col_taps, col_start, c), distance)
        done = jnp.dot(
            whole.reshape(2 * PANEL, 3 * TBLK), band,
            preferred_element_type=jnp.float32, precision=lax.Precision.HIGHEST,
        ).reshape(2, PANEL, TBLK)
        for j in range(nlo):
            cut[c, j] = done[:, j * piece : (j + 1) * piece]
        for k in range(1, nlo):
            cut_copy(c, (l + k) % nlo, l).start()
        plane[c, l] = cut[c, l]

    def left_copy(k):
        return remote(lfilt.at[r], lfilt.at[r], lf_send.at[k], lf_recv.at[r], s, (r + k) % nr)

    def left_arrival(k):
        there = (r + k) % nr
        return remote(lfilt.at[there], lfilt.at[there], lf_send.at[k], lf_recv.at[there], s, there)

    def filter_left():
        pl.when(s > 0)(lambda: left_halo(0, s - 1).wait_recv())
        pl.when(s < n - 1)(lambda: left_halo(1, s + 1).wait_recv())
        shape = (TBLK, TBLK + 2 * HALO)
        distance = lax.broadcasted_iota(jnp.int32, shape, 1) - lax.broadcasted_iota(jnp.int32, shape, 0)
        for b in range(shots // TBLK):
            band = band_of(taps_of(bank, row_taps, row_start, b), distance)
            for part in range(2):
                lfilt[r, part, b * TBLK : (b + 1) * TBLK] = jnp.dot(
                    band, ext[part, b * TBLK : b * TBLK + TBLK + 2 * HALO],
                    preferred_element_type=jnp.float32, precision=lax.Precision.HIGHEST,
                )
        for k in range(1, nr):
            left_copy(k).start()

    def join_left():
        for k in range(1, nr):
            left_arrival(k).wait_recv()
        for j in range(nr):
            high, low = split(lfilt[j])
            lhigh[:, :, j * width : (j + 1) * width] = high
            llow[:, :, j * width : (j + 1) * width] = low

    def up_copy(c, p, shot):
        return remote(upout.at[c, p], upin.at[c, p], up_send.at[c], up_recv.at[c * PANELS + p], shot, r)

    def dn_copy(c, p, shot):
        return remote(dnout.at[c, p], dnin.at[c, p], dn_send.at[c], dn_recv.at[c * PANELS + p], shot, r)

    def mine(c, p):
        place = owner[p] % nlo
        value = plane[c, 0]
        for j in range(1, nlo):
            value = jnp.where(place == j, plane[c, j], value)
        return value

    def side_copy(c, p, there):
        return remote(
            full.at[c, l, p], full.at[c, l, p], side_send.at[c, there], side_recv.at[c, l], h * nlo + there, r
        )

    def side_whole(c, sender, there):
        return remote(
            full.at[c, sender], full.at[c, sender], side_send.at[c, there], side_recv.at[c, sender],
            h * nlo + there, r,
        )

    def move_up(c, p):
        @pl.when(h == 0)
        def _():
            upin[c, p] = jnp.zeros(upin.shape[2:], jnp.float32)

        @pl.when(h > 0)
        def _():
            up_copy(c, p, s - nlo).wait_recv()

        @pl.when(h < nhi - 1)
        def _():
            upout[c, p] = jnp.where(owner[p] // nlo == h, mine(c, p), upin[c, p])
            up_copy(c, p, s + nlo).start()

    def move_down(c, p):
        @pl.when(h == nhi - 1)
        def _():
            dnin[c, p] = jnp.zeros(dnin.shape[2:], jnp.float32)

        @pl.when(h < nhi - 1)
        def _():
            dn_copy(c, p, s + nlo).wait_recv()

        @pl.when(h > 0)
        def _():
            dnout[c, p] = jnp.where(owner[p] // nlo == h, mine(c, p), dnin[c, p])
            dn_copy(c, p, s - nlo).start()

    def settle(c, p):
        line = owner[p] // nlo
        value = jnp.where(line < h, upin[c, p], dnin[c, p])
        full[c, l, p] = jnp.where(line == h, mine(c, p), value)
        for k in range(1, nlo):
            side_copy(c, p, (l + k) % nlo).start()

    def out_copy(c):
        return pltpu.make_async_copy(stage.at[c], out.at[:, :, lanes(c)], out_sem.at[c])

    def product(c):
        for k in range(1, nlo):
            side_whole(c, (l + k) % nlo, l).wait_recv()
        pl.when(c == 0)(join_left)
        pl.when(c == 0)(fetch.wait)
        right = jnp.concatenate(
            [
                jnp.concatenate([full[c, j, p, part] for p in range(PANELS) for j in range(nlo)], axis=0)
                for part in range(2)
            ],
            axis=1,
        )
        high, low = split(right)

        def times(part, rows):
            a, b = lhigh[part, rows], llow[part, rows]
            dot = functools.partial(jnp.dot, preferred_element_type=jnp.float32)
            return dot(a, high) + (dot(a, low) + dot(b, high))

        threshold = level[:, lanes(c)]
        for b in range(shots // (2 * TBLK)):
            rows = slice(b * 2 * TBLK, (b + 1) * 2 * TBLK)
            x, y = times(0, rows), times(1, rows)
            real = rec[0, rows, lanes(c)] - (x[:, :TBLK] - y[:, TBLK:])
            imag = rec[1, rows, lanes(c)] - (x[:, TBLK:] + y[:, :TBLK])
            magnitude = jnp.sqrt(real * real + imag * imag)
            factor = jnp.maximum(magnitude - threshold, 0.0) / jnp.maximum(magnitude, threshold)
            stage[c, 0, rows] = real * factor
            stage[c, 1, rows] = imag * factor
        out_copy(c).start()

    last = HOP * (nhi - 1)
    filter_slab(0)

    def step(k, carry):
        @pl.when((k % PANELS == 0) & (k // PANELS < chunks - 1))
        def _():
            filter_slab(k // PANELS + 1)

        @pl.when((k % PANELS == 0) & (k < items))
        def _():
            for j in range(1, nlo):
                cut_copy(k // PANELS, l, (l + j) % nlo).wait_recv()

        i = k - HOP * h

        @pl.when((i >= 0) & (i < items))
        def _():
            move_up(i // PANELS, i % PANELS)

        j = k - HOP * (nhi - 1 - h)

        @pl.when((j >= 0) & (j < items))
        def _():
            move_down(j // PANELS, j % PANELS)

        m = k - last

        @pl.when((m >= 0) & (m < items))
        def _():
            settle(m // PANELS, m % PANELS)

        q = k - last - SIDE - (PANELS - 1)

        pl.when(k == 1)(filter_left)

        @pl.when((q >= 0) & (q % PANELS == 0))
        def _():
            product(q // PANELS)

        return carry

    lax.fori_loop(0, items + last + SIDE, step, 0)

    pl.when(r < nr - 1)(lambda: slab_halo(0, r + 1).wait_send())
    pl.when(r > 0)(lambda: slab_halo(1, r - 1).wait_send())
    pl.when(s < n - 1)(lambda: left_halo(0, s + 1).wait_send())
    pl.when(s > 0)(lambda: left_halo(1, s - 1).wait_send())
    for k in range(1, nr):
        left_copy(k).wait_send()

    def drain(c, carry):
        for k in range(1, nlo):
            there = (l + k) % nlo
            cut_copy(c, there, l).wait_send()
            side_whole(c, l, there).wait_send()

        @pl.when(h < nhi - 1)
        def _():
            remote(upout.at[c], upin.at[c], up_send.at[c], up_recv.at[0], s + nlo, r).wait_send()

        @pl.when(h > 0)
        def _():
            remote(dnout.at[c], dnin.at[c], dn_send.at[c], dn_recv.at[0], s - nlo, r).wait_send()

        out_copy(c).wait()
        return carry

    lax.fori_loop(0, chunks, drain, 0)


def body(n, nr, data_left, slab_table, recorded, bank, row_taps, row_start, col_taps, col_start, owner, level):
    nlo = 1
    while (2 * nlo) ** 2 <= n and n % (2 * nlo) == 0:
        nlo *= 2
    shots, width = data_left.shape[1], data_left.shape[2]
    columns = slab_table.shape[2]
    chunks = columns // TBLK
    piece = PANEL // nlo
    items = chunks * PANELS
    vmem, smem = pl.BlockSpec(memory_space=pltpu.VMEM), pl.BlockSpec(memory_space=pltpu.SMEM)
    hbm = pl.BlockSpec(memory_space=pl.ANY)
    f32 = jnp.float32
    dma = pltpu.SemaphoreType.DMA
    flow = pltpu.VMEM((chunks, PANELS, 2, piece, TBLK), f32)
    return pl.pallas_call(
        functools.partial(kernel, n, nr, nlo),
        out_shape=jax.ShapeDtypeStruct(recorded.shape, f32),
        in_specs=[vmem, vmem, hbm, vmem] + [smem] * 6,
        out_specs=hbm,
        scratch_shapes=[
            pltpu.VMEM((2, shots + 2 * HALO, width), f32),
            pltpu.VMEM((nr, 2, shots, width), f32),
            pltpu.VMEM((2, shots, nr * width), jnp.bfloat16),
            pltpu.VMEM((2, shots, nr * width), jnp.bfloat16),
            pltpu.VMEM((2, shots, columns), f32),
            pltpu.VMEM((chunks, 2, shots, TBLK), f32),
            pltpu.VMEM((2, 2, PANEL, TBLK), f32),
            pltpu.VMEM((chunks, nlo, 2, piece, TBLK), f32),
            pltpu.VMEM((chunks, nlo, 2, piece, TBLK), f32),
            flow, flow, flow, flow,
            pltpu.VMEM((chunks, nlo, PANELS, 2, piece, TBLK), f32),
            dma, dma((chunks,)), dma((2,)), dma((2,)), dma((2,)), dma((2,)), dma((nr,)), dma((nr,)),
            dma((chunks, nlo)), dma((chunks, nlo)), dma((chunks,)), dma((items,)), dma((chunks,)), dma((items,)),
            dma((chunks, nlo)), dma((chunks, nlo)),
        ],
        compiler_params=pltpu.CompilerParams(
            collective_id=0, has_side_effects=True, vmem_limit_bytes=56 * 2**20
        ),
    )(data_left, slab_table, recorded, level.reshape(1, columns), bank, row_taps, row_start, col_taps, col_start, owner)


def solution(mesh):
    block = P(None, ("freq", "shot"), "rcv")
    return jax.shard_map(
        functools.partial(body, mesh.shape["shot"], mesh.shape["rcv"]),
        mesh=mesh,
        in_specs=(block, block, block, P(), P("shot"), P("shot"), P("rcv"), P("rcv"), P(), P("rcv")),
        out_specs=block,
        check_vma=False,
    )
```

```python
import functools

import jax
import jax.numpy as jnp
from jax import lax
from jax.experimental import pallas as pl
from jax.experimental.pallas import tpu as pltpu
from jax.sharding import PartitionSpec as P

PANEL = 128
PANELS = 4
TAPS = 17
WIN = 13
TBLK = 128
HALO = 8
HOP = 6
SIDE = 4
PARTS = 2
ROUND = PANELS * PARTS
MESH = pl.DeviceIdType.MESH


def taps_of(bank, index, start, block):
    row, first = index[block], start[block]
    return [
        jnp.where((first <= t) & (t < first + WIN), bank[row, t], jnp.float32(0.0))
        for t in range(TAPS)
    ]


def band_of(taps, distance):
    band = jnp.zeros(distance.shape, jnp.float32)
    for t, weight in enumerate(taps):
        band = jnp.where(distance == t, weight, band)
    return band


def split(x):
    high = x.astype(jnp.bfloat16)
    return high, (x - high.astype(jnp.float32)).astype(jnp.bfloat16)


def kernel(
    n, nr, nlo,
    left, slab, recorded, level, bank, row_taps, row_start, col_taps, col_start, owner,
    out,
    ext, lfilt, lhigh, llow, rec, stage, halo, cut, plane, upin, upout, dnin, dnout, full,
    rec_sem, out_sem, lh_send, lh_recv, sh_send, sh_recv, lf_send, lf_recv,
    cut_send, cut_recv, up_send, up_recv, dn_send, dn_recv, side_send, side_recv,
):
    nhi = n // nlo
    shots, width = left.shape[1], left.shape[2]
    columns = slab.shape[2]
    chunks = columns // TBLK
    items = chunks * ROUND
    piece = PANEL // nlo
    s, r = lax.axis_index("shot"), lax.axis_index("rcv")
    h, l = s // nlo, s % nlo

    def at(shot, rcv):
        return (lax.axis_index("freq"), shot, rcv)

    def remote(src, dst, send, recv, shot, rcv):
        return pltpu.make_async_remote_copy(
            src_ref=src, dst_ref=dst, send_sem=send, recv_sem=recv,
            device_id=at(shot, rcv), device_id_type=MESH,
        )

    barrier = pltpu.get_barrier_semaphore()

    def greet(shot, rcv):
        pl.semaphore_signal(barrier, inc=1, device_id=at(shot, rcv), device_id_type=MESH)

    for k in range(1, nr):
        greet(s, (r + k) % nr)
    for k in range(1, nlo):
        greet(h * nlo + (l + k) % nlo, r)
    pl.when(h > 0)(lambda: greet(s - nlo, r))
    pl.when(h < nhi - 1)(lambda: greet(s + nlo, r))
    pl.when(s > 0)(lambda: greet(s - 1, r))
    pl.when(s < n - 1)(lambda: greet(s + 1, r))
    ends = jnp.int32(nr + nlo - 2)
    for near in (h > 0, h < nhi - 1, s > 0, s < n - 1):
        ends = ends + jnp.where(near, 1, 0)
    pl.semaphore_wait(barrier, ends)

    def slab_halo(to, rcv):
        start = columns - TBLK if to == 0 else 0
        return remote(slab.at[:, :, pl.ds(start, TBLK)], halo.at[to], sh_send.at[to], sh_recv.at[to], s, rcv)

    def left_halo(to, shot):
        start = shots - HALO if to == 0 else 0
        place = 0 if to == 0 else shots + HALO
        return remote(
            left.at[:, pl.ds(start, HALO)], ext.at[:, pl.ds(place, HALO)],
            lh_send.at[to], lh_recv.at[to], shot, r,
        )

    pl.when(r < nr - 1)(lambda: slab_halo(0, r + 1).start())
    pl.when(r > 0)(lambda: slab_halo(1, r - 1).start())
    pl.when(s < n - 1)(lambda: left_halo(0, s + 1).start())
    pl.when(s > 0)(lambda: left_halo(1, s - 1).start())
    fetch = pltpu.make_async_copy(recorded, rec, rec_sem)
    fetch.start()

    @pl.when(r == 0)
    def _():
        halo[0] = jnp.zeros(halo.shape[1:], jnp.float32)

    @pl.when(r == nr - 1)
    def _():
        halo[1] = jnp.zeros(halo.shape[1:], jnp.float32)

    @pl.when(s == 0)
    def _():
        ext[:, :HALO] = jnp.zeros((2, HALO, width), jnp.float32)

    @pl.when(s == n - 1)
    def _():
        ext[:, shots + HALO :] = jnp.zeros((2, HALO, width), jnp.float32)

    ext[:, HALO : shots + HALO] = left[...]
    pl.when(r > 0)(lambda: slab_halo(0, r - 1).wait_recv())
    pl.when(r < nr - 1)(lambda: slab_halo(1, r + 1).wait_recv())

    def lanes(c):
        return pl.ds(pl.multiple_of(c * TBLK, TBLK), TBLK)

    def cut_copy(c, there, sender):
        return remote(
            cut.at[c, there], plane.at[c, sender], cut_send.at[c, there], cut_recv.at[c, sender],
            h * nlo + there, r,
        )

    def filter_slab(c):
        before = jnp.where(c > 0, slab[:, :, lanes(jnp.maximum(c - 1, 0))], halo[0])
        after = jnp.where(c < chunks - 1, slab[:, :, lanes(jnp.minimum(c + 1, chunks - 1))], halo[1])
        whole = jnp.concatenate([before, slab[:, :, lanes(c)], after], axis=2)
        shape = (3 * TBLK, TBLK)
        distance = (
            lax.broadcasted_iota(jnp.int32, shape, 0) - lax.broadcasted_iota(jnp.int32, shape, 1) - (TBLK - HALO)
        )
        band = band_of(taps_of(bank, col_taps, col_start, c), distance)
        done = jnp.dot(
            whole.reshape(2 * PANEL, 3 * TBLK), band,
            preferred_element_type=jnp.float32, precision=lax.Precision.HIGHEST,
        ).reshape(2, PANEL, TBLK)
        for j in range(nlo):
            cut[c, j] = done[:, j * piece : (j + 1) * piece]
        for k in range(1, nlo):
            cut_copy(c, (l + k) % nlo, l).start()
        plane[c, l] = cut[c, l]

    def left_copy(k):
        return remote(lfilt.at[r], lfilt.at[r], lf_send.at[k], lf_recv.at[r], s, (r + k) % nr)

    def left_arrival(k):
        there = (r + k) % nr
        return remote(lfilt.at[there], lfilt.at[there], lf_send.at[k], lf_recv.at[there], s, there)

    def filter_left():
        pl.when(s > 0)(lambda: left_halo(0, s - 1).wait_recv())
        pl.when(s < n - 1)(lambda: left_halo(1, s + 1).wait_recv())
        shape = (TBLK, TBLK + 2 * HALO)
        distance = lax.broadcasted_iota(jnp.int32, shape, 1) - lax.broadcasted_iota(jnp.int32, shape, 0)
        for b in range(shots // TBLK):
            band = band_of(taps_of(bank, row_taps, row_start, b), distance)
            for part in range(2):
                lfilt[r, part, b * TBLK : (b + 1) * TBLK] = jnp.dot(
                    band, ext[part, b * TBLK : b * TBLK + TBLK + 2 * HALO],
                    preferred_element_type=jnp.float32, precision=lax.Precision.HIGHEST,
                )
        for k in range(1, nr):
            left_copy(k).start()

    def join_left():
        for k in range(1, nr):
            left_arrival(k).wait_recv()
        for j in range(nr):
            high, low = split(lfilt[j])
            lhigh[:, :, j * width : (j + 1) * width] = high
            llow[:, :, j * width : (j + 1) * width] = low

    def up_copy(c, p, part, shot):
        return remote(
            upout.at[c, p, part], upin.at[c, p, part], up_send.at[c],
            up_recv.at[c * ROUND + p * PARTS + part], shot, r,
        )

    def dn_copy(c, p, part, shot):
        return remote(
            dnout.at[c, p, part], dnin.at[c, p, part], dn_send.at[c],
            dn_recv.at[c * ROUND + p * PARTS + part], shot, r,
        )

    def mine(c, p, part):
        place = owner[p] % nlo
        value = plane[c, 0, part]
        for j in range(1, nlo):
            value = jnp.where(place == j, plane[c, j, part], value)
        return value

    def side_copy(c, p, part, there):
        return remote(
            full.at[c, l, p, part], full.at[c, l, p, part], side_send.at[c, there], side_recv.at[c, l], h * nlo + there, r
        )

    def side_whole(c, sender, there):
        return remote(
            full.at[c, sender], full.at[c, sender], side_send.at[c, there], side_recv.at[c, sender],
            h * nlo + there, r,
        )

    def move_up(c, p, part):
        @pl.when(h == 0)
        def _():
            upin[c, p, part] = jnp.zeros(upin.shape[3:], jnp.float32)

        @pl.when(h > 0)
        def _():
            up_copy(c, p, part, s - nlo).wait_recv()

        @pl.when(h < nhi - 1)
        def _():
            upout[c, p, part] = jnp.where(owner[p] // nlo == h, mine(c, p, part), upin[c, p, part])
            up_copy(c, p, part, s + nlo).start()

    def move_down(c, p, part):
        @pl.when(h == nhi - 1)
        def _():
            dnin[c, p, part] = jnp.zeros(dnin.shape[3:], jnp.float32)

        @pl.when(h < nhi - 1)
        def _():
            dn_copy(c, p, part, s + nlo).wait_recv()

        @pl.when(h > 0)
        def _():
            dnout[c, p, part] = jnp.where(owner[p] // nlo == h, mine(c, p, part), dnin[c, p, part])
            dn_copy(c, p, part, s - nlo).start()

    def settle(c, p, part):
        line = owner[p] // nlo
        value = jnp.where(line < h, upin[c, p, part], dnin[c, p, part])
        full[c, l, p, part] = jnp.where(line == h, mine(c, p, part), value)
        for k in range(1, nlo):
            side_copy(c, p, part, (l + k) % nlo).start()

    def out_copy(c):
        return pltpu.make_async_copy(stage.at[c], out.at[:, :, lanes(c)], out_sem.at[c])

    def product(c):
        for k in range(1, nlo):
            side_whole(c, (l + k) % nlo, l).wait_recv()
        pl.when(c == 0)(join_left)
        pl.when(c == 0)(fetch.wait)
        right = jnp.concatenate(
            [
                jnp.concatenate([full[c, j, p, part] for p in range(PANELS) for j in range(nlo)], axis=0)
                for part in range(2)
            ],
            axis=1,
        )
        high, low = split(right)

        def times(part, rows):
            a, b = lhigh[part, rows], llow[part, rows]
            dot = functools.partial(jnp.dot, preferred_element_type=jnp.float32)
            return dot(a, high) + (dot(a, low) + dot(b, high))

        threshold = level[:, lanes(c)]
        for b in range(shots // (2 * TBLK)):
            rows = slice(b * 2 * TBLK, (b + 1) * 2 * TBLK)
            x, y = times(0, rows), times(1, rows)
            real = rec[0, rows, lanes(c)] - (x[:, :TBLK] - y[:, TBLK:])
            imag = rec[1, rows, lanes(c)] - (x[:, TBLK:] + y[:, :TBLK])
            magnitude = jnp.sqrt(real * real + imag * imag)
            factor = jnp.maximum(magnitude - threshold, 0.0) / jnp.maximum(magnitude, threshold)
            stage[c, 0, rows] = real * factor
            stage[c, 1, rows] = imag * factor
        out_copy(c).start()

    last = HOP * (nhi - 1)
    filter_slab(0)

    def step(k, carry):
        @pl.when(k < chunks - 1)
        def _():
            filter_slab(k + 1)

        pl.when(k == 0)(filter_left)

        @pl.when((k % ROUND == 0) & (k < items))
        def _():
            for j in range(1, nlo):
                cut_copy(k // ROUND, l, (l + j) % nlo).wait_recv()

        i = k - HOP * h

        @pl.when((i >= 0) & (i < items))
        def _():
            move_up(i // ROUND, i // PARTS % PANELS, i % PARTS)

        j = k - HOP * (nhi - 1 - h)

        @pl.when((j >= 0) & (j < items))
        def _():
            move_down(j // ROUND, j // PARTS % PANELS, j % PARTS)

        m = k - last

        @pl.when((m >= 0) & (m < items))
        def _():
            settle(m // ROUND, m // PARTS % PANELS, m % PARTS)

        q = k - last - SIDE - (ROUND - 1)

        @pl.when((q >= 0) & (q % ROUND == 0))
        def _():
            product(q // ROUND)

        return carry

    lax.fori_loop(0, items + last + SIDE, step, 0)

    pl.when(r < nr - 1)(lambda: slab_halo(0, r + 1).wait_send())
    pl.when(r > 0)(lambda: slab_halo(1, r - 1).wait_send())
    pl.when(s < n - 1)(lambda: left_halo(0, s + 1).wait_send())
    pl.when(s > 0)(lambda: left_halo(1, s - 1).wait_send())
    for k in range(1, nr):
        left_copy(k).wait_send()

    def drain(c, carry):
        for k in range(1, nlo):
            there = (l + k) % nlo
            cut_copy(c, there, l).wait_send()
            side_whole(c, l, there).wait_send()

        @pl.when(h < nhi - 1)
        def _():
            remote(upout.at[c], upin.at[c], up_send.at[c], up_recv.at[0], s + nlo, r).wait_send()

        @pl.when(h > 0)
        def _():
            remote(dnout.at[c], dnin.at[c], dn_send.at[c], dn_recv.at[0], s - nlo, r).wait_send()

        out_copy(c).wait()
        return carry

    lax.fori_loop(0, chunks, drain, 0)


def body(n, nr, data_left, slab_table, recorded, bank, row_taps, row_start, col_taps, col_start, owner, level):
    nlo = 1
    while (2 * nlo) ** 2 <= n and n % (2 * nlo) == 0:
        nlo *= 2
    shots, width = data_left.shape[1], data_left.shape[2]
    columns = slab_table.shape[2]
    chunks = columns // TBLK
    piece = PANEL // nlo
    items = chunks * ROUND
    vmem, smem = pl.BlockSpec(memory_space=pltpu.VMEM), pl.BlockSpec(memory_space=pltpu.SMEM)
    hbm = pl.BlockSpec(memory_space=pl.ANY)
    f32 = jnp.float32
    dma = pltpu.SemaphoreType.DMA
    flow = pltpu.VMEM((chunks, PANELS, 2, piece, TBLK), f32)
    return pl.pallas_call(
        functools.partial(kernel, n, nr, nlo),
        out_shape=jax.ShapeDtypeStruct(recorded.shape, f32),
        in_specs=[vmem, vmem, hbm, vmem] + [smem] * 6,
        out_specs=hbm,
        scratch_shapes=[
            pltpu.VMEM((2, shots + 2 * HALO, width), f32),
            pltpu.VMEM((nr, 2, shots, width), f32),
            pltpu.VMEM((2, shots, nr * width), jnp.bfloat16),
            pltpu.VMEM((2, shots, nr * width), jnp.bfloat16),
            pltpu.VMEM((2, shots, columns), f32),
            pltpu.VMEM((chunks, 2, shots, TBLK), f32),
            pltpu.VMEM((2, 2, PANEL, TBLK), f32),
            pltpu.VMEM((chunks, nlo, 2, piece, TBLK), f32),
            pltpu.VMEM((chunks, nlo, 2, piece, TBLK), f32),
            flow, flow, flow, flow,
            pltpu.VMEM((chunks, nlo, PANELS, 2, piece, TBLK), f32),
            dma, dma((chunks,)), dma((2,)), dma((2,)), dma((2,)), dma((2,)), dma((nr,)), dma((nr,)),
            dma((chunks, nlo)), dma((chunks, nlo)), dma((chunks,)), dma((items,)), dma((chunks,)), dma((items,)),
            dma((chunks, nlo)), dma((chunks, nlo)),
        ],
        compiler_params=pltpu.CompilerParams(
            collective_id=0, has_side_effects=True, vmem_limit_bytes=56 * 2**20
        ),
    )(data_left, slab_table, recorded, level.reshape(1, columns), bank, row_taps, row_start, col_taps, col_start, owner)


def solution(mesh):
    block = P(None, ("freq", "shot"), "rcv")
    return jax.shard_map(
        functools.partial(body, mesh.shape["shot"], mesh.shape["rcv"]),
        mesh=mesh,
        in_specs=(block, block, block, P(), P("shot"), P("shot"), P("rcv"), P("rcv"), P(), P("rcv")),
        out_specs=block,
        check_vma=False,
    )
```

```python
import functools

import jax
import jax.numpy as jnp
from jax import lax
from jax.experimental import pallas as pl
from jax.experimental.pallas import tpu as pltpu
from jax.sharding import PartitionSpec as P

PANEL = 128
PANELS = 4
TAPS = 17
WIN = 13
TBLK = 128
HALO = 8
HOP = 6
SIDE = 8
PARTS = 2
ROUND = PANELS * PARTS
MESH = pl.DeviceIdType.MESH


def taps_of(bank, index, start, block):
    row, first = index[block], start[block]
    return [
        jnp.where((first <= t) & (t < first + WIN), bank[row, t], jnp.float32(0.0))
        for t in range(TAPS)
    ]


def band_of(taps, distance):
    band = jnp.zeros(distance.shape, jnp.float32)
    for t, weight in enumerate(taps):
        band = jnp.where(distance == t, weight, band)
    return band


def split(x):
    high = x.astype(jnp.bfloat16)
    return high, (x - high.astype(jnp.float32)).astype(jnp.bfloat16)


def kernel(
    n, nr, nlo,
    left, slab, recorded, level, bank, row_taps, row_start, col_taps, col_start, owner,
    out,
    ext, lfilt, lhigh, llow, rec, stage, halo, cut, plane, upin, upout, dnin, dnout, full,
    rec_sem, out_sem, lh_send, lh_recv, sh_send, sh_recv, lf_send, lf_recv,
    cut_send, cut_recv, up_send, up_recv, dn_send, dn_recv, side_send, side_recv,
):
    nhi = n // nlo
    shots, width = left.shape[1], left.shape[2]
    columns = slab.shape[2]
    chunks = columns // TBLK
    items = chunks * ROUND
    piece = PANEL // nlo
    s, r = lax.axis_index("shot"), lax.axis_index("rcv")
    h, l = s // nlo, s % nlo

    def at(shot, rcv):
        return (lax.axis_index("freq"), shot, rcv)

    def remote(src, dst, send, recv, shot, rcv):
        return pltpu.make_async_remote_copy(
            src_ref=src, dst_ref=dst, send_sem=send, recv_sem=recv,
            device_id=at(shot, rcv), device_id_type=MESH,
        )

    barrier = pltpu.get_barrier_semaphore()

    def greet(shot, rcv):
        pl.semaphore_signal(barrier, inc=1, device_id=at(shot, rcv), device_id_type=MESH)

    for k in range(1, nr):
        greet(s, (r + k) % nr)
    for k in range(1, nlo):
        greet(h * nlo + (l + k) % nlo, r)
    pl.when(h > 0)(lambda: greet(s - nlo, r))
    pl.when(h < nhi - 1)(lambda: greet(s + nlo, r))
    pl.when(s > 0)(lambda: greet(s - 1, r))
    pl.when(s < n - 1)(lambda: greet(s + 1, r))
    ends = jnp.int32(nr + nlo - 2)
    for near in (h > 0, h < nhi - 1, s > 0, s < n - 1):
        ends = ends + jnp.where(near, 1, 0)
    pl.semaphore_wait(barrier, ends)

    def slab_halo(to, rcv):
        start = columns - TBLK if to == 0 else 0
        return remote(slab.at[:, :, pl.ds(start, TBLK)], halo.at[to], sh_send.at[to], sh_recv.at[to], s, rcv)

    def left_halo(to, shot):
        start = shots - HALO if to == 0 else 0
        place = 0 if to == 0 else shots + HALO
        return remote(
            left.at[:, pl.ds(start, HALO)], ext.at[:, pl.ds(place, HALO)],
            lh_send.at[to], lh_recv.at[to], shot, r,
        )

    pl.when(r < nr - 1)(lambda: slab_halo(0, r + 1).start())
    pl.when(r > 0)(lambda: slab_halo(1, r - 1).start())
    pl.when(s < n - 1)(lambda: left_halo(0, s + 1).start())
    pl.when(s > 0)(lambda: left_halo(1, s - 1).start())
    fetch = pltpu.make_async_copy(recorded, rec, rec_sem)
    fetch.start()

    @pl.when(r == 0)
    def _():
        halo[0] = jnp.zeros(halo.shape[1:], jnp.float32)

    @pl.when(r == nr - 1)
    def _():
        halo[1] = jnp.zeros(halo.shape[1:], jnp.float32)

    @pl.when(s == 0)
    def _():
        ext[:, :HALO] = jnp.zeros((2, HALO, width), jnp.float32)

    @pl.when(s == n - 1)
    def _():
        ext[:, shots + HALO :] = jnp.zeros((2, HALO, width), jnp.float32)

    ext[:, HALO : shots + HALO] = left[...]
    pl.when(r > 0)(lambda: slab_halo(0, r - 1).wait_recv())
    pl.when(r < nr - 1)(lambda: slab_halo(1, r + 1).wait_recv())

    def lanes(c):
        return pl.ds(pl.multiple_of(c * TBLK, TBLK), TBLK)

    def cut_copy(c, there, sender):
        return remote(
            cut.at[c, there], plane.at[c, sender], cut_send.at[c, there], cut_recv.at[c, sender],
            h * nlo + there, r,
        )

    def filter_slab(c):
        before = jnp.where(c > 0, slab[:, :, lanes(jnp.maximum(c - 1, 0))], halo[0])
        after = jnp.where(c < chunks - 1, slab[:, :, lanes(jnp.minimum(c + 1, chunks - 1))], halo[1])
        whole = jnp.concatenate([before, slab[:, :, lanes(c)], after], axis=2)
        shape = (3 * TBLK, TBLK)
        distance = (
            lax.broadcasted_iota(jnp.int32, shape, 0) - lax.broadcasted_iota(jnp.int32, shape, 1) - (TBLK - HALO)
        )
        band = band_of(taps_of(bank, col_taps, col_start, c), distance)
        done = jnp.dot(
            whole.reshape(2 * PANEL, 3 * TBLK), band,
            preferred_element_type=jnp.float32, precision=lax.Precision.HIGHEST,
        ).reshape(2, PANEL, TBLK)
        for j in range(nlo):
            cut[c, j] = done[:, j * piece : (j + 1) * piece]
        for k in range(1, nlo):
            cut_copy(c, (l + k) % nlo, l).start()
        plane[c, l] = cut[c, l]

    def left_copy(k):
        return remote(lfilt.at[r], lfilt.at[r], lf_send.at[k], lf_recv.at[r], s, (r + k) % nr)

    def left_arrival(k):
        there = (r + k) % nr
        return remote(lfilt.at[there], lfilt.at[there], lf_send.at[k], lf_recv.at[there], s, there)

    def filter_left():
        pl.when(s > 0)(lambda: left_halo(0, s - 1).wait_recv())
        pl.when(s < n - 1)(lambda: left_halo(1, s + 1).wait_recv())
        shape = (TBLK, TBLK + 2 * HALO)
        distance = lax.broadcasted_iota(jnp.int32, shape, 1) - lax.broadcasted_iota(jnp.int32, shape, 0)
        for b in range(shots // TBLK):
            band = band_of(taps_of(bank, row_taps, row_start, b), distance)
            for part in range(2):
                lfilt[r, part, b * TBLK : (b + 1) * TBLK] = jnp.dot(
                    band, ext[part, b * TBLK : b * TBLK + TBLK + 2 * HALO],
                    preferred_element_type=jnp.float32, precision=lax.Precision.HIGHEST,
                )
        for k in range(1, nr):
            left_copy(k).start()

    def join_left():
        for k in range(1, nr):
            left_arrival(k).wait_recv()
        for j in range(nr):
            high, low = split(lfilt[j])
            lhigh[:, :, j * width : (j + 1) * width] = high
            llow[:, :, j * width : (j + 1) * width] = low

    def up_copy(c, p, part, shot):
        return remote(
            upout.at[c, p, part], upin.at[c, p, part], up_send.at[c],
            up_recv.at[c * ROUND + p * PARTS + part], shot, r,
        )

    def dn_copy(c, p, part, shot):
        return remote(
            dnout.at[c, p, part], dnin.at[c, p, part], dn_send.at[c],
            dn_recv.at[c * ROUND + p * PARTS + part], shot, r,
        )

    def mine(c, p, part):
        place = owner[p] % nlo
        value = plane[c, 0, part]
        for j in range(1, nlo):
            value = jnp.where(place == j, plane[c, j, part], value)
        return value

    def side_copy(c, p, part, there):
        return remote(
            full.at[c, l, p, part], full.at[c, l, p, part], side_send.at[c, there], side_recv.at[c, l], h * nlo + there, r
        )

    def side_whole(c, sender, there):
        return remote(
            full.at[c, sender], full.at[c, sender], side_send.at[c, there], side_recv.at[c, sender],
            h * nlo + there, r,
        )

    def move_up(c, p, part):
        @pl.when(h == 0)
        def _():
            upin[c, p, part] = jnp.zeros(upin.shape[3:], jnp.float32)

        @pl.when(h > 0)
        def _():
            up_copy(c, p, part, s - nlo).wait_recv()

        @pl.when(h < nhi - 1)
        def _():
            upout[c, p, part] = jnp.where(owner[p] // nlo == h, mine(c, p, part), upin[c, p, part])
            up_copy(c, p, part, s + nlo).start()

    def move_down(c, p, part):
        @pl.when(h == nhi - 1)
        def _():
            dnin[c, p, part] = jnp.zeros(dnin.shape[3:], jnp.float32)

        @pl.when(h < nhi - 1)
        def _():
            dn_copy(c, p, part, s + nlo).wait_recv()

        @pl.when(h > 0)
        def _():
            dnout[c, p, part] = jnp.where(owner[p] // nlo == h, mine(c, p, part), dnin[c, p, part])
            dn_copy(c, p, part, s - nlo).start()

    def settle(c, p, part):
        line = owner[p] // nlo
        value = jnp.where(line < h, upin[c, p, part], dnin[c, p, part])
        full[c, l, p, part] = jnp.where(line == h, mine(c, p, part), value)
        for k in range(1, nlo):
            side_copy(c, p, part, (l + k) % nlo).start()

    def out_copy(c):
        return pltpu.make_async_copy(stage.at[c], out.at[:, :, lanes(c)], out_sem.at[c])

    def product(c):
        for k in range(1, nlo):
            side_whole(c, (l + k) % nlo, l).wait_recv()
        pl.when(c == 0)(join_left)
        pl.when(c == 0)(fetch.wait)
        right = jnp.concatenate(
            [
                jnp.concatenate([full[c, j, p, part] for p in range(PANELS) for j in range(nlo)], axis=0)
                for part in range(2)
            ],
            axis=1,
        )
        high, low = split(right)

        def times(part, rows):
            a, b = lhigh[part, rows], llow[part, rows]
            dot = functools.partial(jnp.dot, preferred_element_type=jnp.float32)
            return dot(a, high) + (dot(a, low) + dot(b, high))

        threshold = level[:, lanes(c)]
        for b in range(shots // (2 * TBLK)):
            rows = slice(b * 2 * TBLK, (b + 1) * 2 * TBLK)
            x, y = times(0, rows), times(1, rows)
            real = rec[0, rows, lanes(c)] - (x[:, :TBLK] - y[:, TBLK:])
            imag = rec[1, rows, lanes(c)] - (x[:, TBLK:] + y[:, :TBLK])
            magnitude = jnp.sqrt(real * real + imag * imag)
            factor = jnp.maximum(magnitude - threshold, 0.0) / jnp.maximum(magnitude, threshold)
            stage[c, 0, rows] = real * factor
            stage[c, 1, rows] = imag * factor
        out_copy(c).start()

    last = HOP * (nhi - 1)
    filter_slab(0)

    def step(k, carry):
        @pl.when(k < chunks - 1)
        def _():
            filter_slab(k + 1)

        pl.when(k == 0)(filter_left)

        @pl.when((k % ROUND == 0) & (k < items))
        def _():
            for j in range(1, nlo):
                cut_copy(k // ROUND, l, (l + j) % nlo).wait_recv()

        i = k - HOP * h

        @pl.when((i >= 0) & (i < items))
        def _():
            move_up(i // ROUND, i // PARTS % PANELS, i % PARTS)

        j = k - HOP * (nhi - 1 - h)

        @pl.when((j >= 0) & (j < items))
        def _():
            move_down(j // ROUND, j // PARTS % PANELS, j % PARTS)

        m = k - HOP * jnp.maximum(h, nhi - 1 - h)

        @pl.when((m >= 0) & (m < items))
        def _():
            settle(m // ROUND, m // PARTS % PANELS, m % PARTS)

        q = k - last - SIDE - (ROUND - 1)

        @pl.when((q >= 0) & (q % ROUND == 0))
        def _():
            product(q // ROUND)

        return carry

    lax.fori_loop(0, items + last + SIDE, step, 0)

    pl.when(r < nr - 1)(lambda: slab_halo(0, r + 1).wait_send())
    pl.when(r > 0)(lambda: slab_halo(1, r - 1).wait_send())
    pl.when(s < n - 1)(lambda: left_halo(0, s + 1).wait_send())
    pl.when(s > 0)(lambda: left_halo(1, s - 1).wait_send())
    for k in range(1, nr):
        left_copy(k).wait_send()

    def drain(c, carry):
        for k in range(1, nlo):
            there = (l + k) % nlo
            cut_copy(c, there, l).wait_send()
            side_whole(c, l, there).wait_send()

        @pl.when(h < nhi - 1)
        def _():
            remote(upout.at[c], upin.at[c], up_send.at[c], up_recv.at[0], s + nlo, r).wait_send()

        @pl.when(h > 0)
        def _():
            remote(dnout.at[c], dnin.at[c], dn_send.at[c], dn_recv.at[0], s - nlo, r).wait_send()

        out_copy(c).wait()
        return carry

    lax.fori_loop(0, chunks, drain, 0)


def body(n, nr, data_left, slab_table, recorded, bank, row_taps, row_start, col_taps, col_start, owner, level):
    nlo = 1
    while (2 * nlo) ** 2 <= n and n % (2 * nlo) == 0:
        nlo *= 2
    shots, width = data_left.shape[1], data_left.shape[2]
    columns = slab_table.shape[2]
    chunks = columns // TBLK
    piece = PANEL // nlo
    items = chunks * ROUND
    vmem, smem = pl.BlockSpec(memory_space=pltpu.VMEM), pl.BlockSpec(memory_space=pltpu.SMEM)
    hbm = pl.BlockSpec(memory_space=pl.ANY)
    f32 = jnp.float32
    dma = pltpu.SemaphoreType.DMA
    flow = pltpu.VMEM((chunks, PANELS, 2, piece, TBLK), f32)
    return pl.pallas_call(
        functools.partial(kernel, n, nr, nlo),
        out_shape=jax.ShapeDtypeStruct(recorded.shape, f32),
        in_specs=[vmem, vmem, hbm, vmem] + [smem] * 6,
        out_specs=hbm,
        scratch_shapes=[
            pltpu.VMEM((2, shots + 2 * HALO, width), f32),
            pltpu.VMEM((nr, 2, shots, width), f32),
            pltpu.VMEM((2, shots, nr * width), jnp.bfloat16),
            pltpu.VMEM((2, shots, nr * width), jnp.bfloat16),
            pltpu.VMEM((2, shots, columns), f32),
            pltpu.VMEM((chunks, 2, shots, TBLK), f32),
            pltpu.VMEM((2, 2, PANEL, TBLK), f32),
            pltpu.VMEM((chunks, nlo, 2, piece, TBLK), f32),
            pltpu.VMEM((chunks, nlo, 2, piece, TBLK), f32),
            flow, flow, flow, flow,
            pltpu.VMEM((chunks, nlo, PANELS, 2, piece, TBLK), f32),
            dma, dma((chunks,)), dma((2,)), dma((2,)), dma((2,)), dma((2,)), dma((nr,)), dma((nr,)),
            dma((chunks, nlo)), dma((chunks, nlo)), dma((chunks,)), dma((items,)), dma((chunks,)), dma((items,)),
            dma((chunks, nlo)), dma((chunks, nlo)),
        ],
        compiler_params=pltpu.CompilerParams(
            collective_id=0, has_side_effects=True, vmem_limit_bytes=56 * 2**20
        ),
    )(data_left, slab_table, recorded, level.reshape(1, columns), bank, row_taps, row_start, col_taps, col_start, owner)


def solution(mesh):
    block = P(None, ("freq", "shot"), "rcv")
    return jax.shard_map(
        functools.partial(body, mesh.shape["shot"], mesh.shape["rcv"]),
        mesh=mesh,
        in_specs=(block, block, block, P(), P("shot"), P("shot"), P("rcv"), P("rcv"), P(), P("rcv")),
        out_specs=block,
        check_vma=False,
    )
```
